128 devices in a mesh: seq: 32 (over z, y, core), tp: 4 (over x).
Axes of the slice: x: 4, y: 4, z: 4, core: 2. Of those that a mesh axis runs over, the one named last changes fastest.
Arguments:
- query_proj: bfloat16 [6144, 3072], P('seq', 'tp'), may hold values from -6 to 6
- key_proj: bfloat16 [6144, 3072], P('seq', 'tp'), may hold values from -6 to 6
- value_proj: bfloat16 [6144, 3072], P('seq', 'tp'), may hold values from -6 to 6
- attn_output: bfloat16 [6144, 3072], P('seq', 'tp')
- out_grad: bfloat16 [6144, 3072], P('seq', 'tp'), may hold values from -6 to 6
- log_norm: float32 [6144, 24], P('seq', 'tp')
- router_logit: float32 [6144], P('seq'), may hold values from -4 to 4
- keep_positions: int32 [6144], replicated, may hold values from -1 to 32767, as said below
Outputs:
- query_grad: bfloat16 [6144, 3072], P('seq', 'tp')
- key_grad: bfloat16 [6144, 3072], P('seq', 'tp')
- value_grad: bfloat16 [6144, 3072], P('seq', 'tp')
- router_grad: float32 [6144], P('seq')
The draws below stay inside these ranges and needn't reach their ends.
Inputs may be any that keep to these rules, and one draw needn't show every extreme that they name: `keep_positions`: slots s*192 to (s+1)*192 - 1 hold the kept positions of tokens s*1024 to (s+1)*1024 - 1 in increasing order, followed by -1 in the unused slots. Exactly 4096 tokens are kept in all; some shard fills all 192 slots and some shard keeps only 64.
All inputs are finite; a program needn't handle non-finite values.
Results may differ from the reference program's by a relative error of at most 0.03.
Values may be sent and summed in bfloat16 or wider, within the bound.
A program may use at most 128 MiB of HBM per device.

```python
import jax
import jax.numpy as jnp
from jax import lax

SLOTS = 192
HEADS = 24
HEAD_DIM = 128
WIDTH = 3072
TOK_SHARD = 1024
KEPT_SLOTS = 6144
N_SEQ = 32


def kept_positions(key):
    third = SLOTS // 3
    middle = 2 * third
    first_key, second_key, third_key = jax.random.split(key, 3)
    order = jax.random.permutation(first_key, N_SEQ)
    offsets = jax.random.randint(second_key, (N_SEQ // 2,), -(third - 1), third)
    offsets = offsets.at[0].set(third)
    paired = jnp.stack([middle + offsets, middle - offsets], axis=1).reshape(N_SEQ)
    counts = jnp.zeros((N_SEQ,), jnp.int32).at[order].set(paired.astype(jnp.int32))
    shard_keys = jax.random.split(third_key, N_SEQ)

    def one_shard(shard_key, shard, count):
        ranking = jax.random.permutation(shard_key, TOK_SHARD)
        local = jnp.arange(TOK_SHARD, dtype=jnp.int32)
        chosen = jnp.where(ranking < count, local, TOK_SHARD + local)
        ordered = jnp.sort(chosen)[:SLOTS]
        return jnp.where(ordered < TOK_SHARD, ordered + shard * TOK_SHARD, -1)
    result = jax.vmap(one_shard)(shard_keys, jnp.arange(N_SEQ, dtype=jnp.int32), counts)
    return result.reshape(N_SEQ * SLOTS).astype(jnp.int32)


def draw_keep_positions(key, part):
    return kept_positions(key)


def draw_log_norm(key, part):
    positions = kept_positions(key)
    key = jax.random.fold_in(key, 7)
    valid = positions >= 0
    ranks = jnp.cumsum(valid.astype(jnp.int32))
    base = jnp.where(valid, jnp.log(jnp.maximum(ranks, 1).astype(jnp.float32)) + 0.5, 0.0)
    noise = jax.random.uniform(key, (KEPT_SLOTS, HEADS), jnp.float32, -0.3, 0.3)
    return (base[:, None] + noise).astype(jnp.float32)


def draw_attn_output(key, part):
    key = jax.random.fold_in(key, 11)
    columns = jnp.arange(WIDTH, dtype=jnp.float32) / (WIDTH - 1)
    column_scale = 0.1 * jnp.power(3.0, columns)
    values = jax.random.normal(key, (KEPT_SLOTS, WIDTH), jnp.float32)
    return (values * column_scale).astype(jnp.bfloat16)


def block_scale(own_key, shape, cuts, smallest, largest):
    factor_of = 1.0
    for dim, blocks in cuts:
        heights = jax.random.uniform(jax.random.fold_in(jax.random.fold_in(own_key, 6), dim), (blocks,), jnp.float32, smallest / len(cuts), largest / len(cuts))
        factor_of = factor_of * jnp.repeat(jnp.exp(heights), shape[dim] // blocks).reshape((-1,) + (1,) * (len(shape) - 1 - dim))
    return factor_of


def gaussian(stream_key, shape, width, most, cuts=(), kind=jnp.bfloat16):
    gain = block_scale(stream_key, shape, cuts, -0.22, 0.18) if cuts else 1.0
    entries = jax.random.normal(stream_key, shape, jnp.float32) * width * gain
    return jnp.minimum(jnp.maximum(entries, -most), most).astype(kind)


def setup_inputs(seed: int = 0) -> dict:
    keys = jax.random.split(jax.random.key(seed), 9)
    return {
        "query_proj": gaussian(keys[0], (KEPT_SLOTS, WIDTH), 1.0, 6.0, ((0, 32), (1, 4))),
        "key_proj": gaussian(keys[1], (KEPT_SLOTS, WIDTH), 1.0, 6.0, ((0, 32), (1, 4))),
        "value_proj": gaussian(keys[2], (KEPT_SLOTS, WIDTH), 1.0, 6.0, ((0, 32), (1, 4))),
        "attn_output": draw_attn_output(jax.random.fold_in(keys[8], 71), 0),
        "out_grad": gaussian(keys[4], (KEPT_SLOTS, WIDTH), 1.0, 6.0, ((0, 32), (1, 4))),
        "log_norm": draw_log_norm(jax.random.fold_in(keys[8], 71), 0),
        "router_logit": gaussian(keys[6], (KEPT_SLOTS,), 1.5, 4.0, ((0, 32),), jnp.float32),
        "keep_positions": draw_keep_positions(jax.random.fold_in(keys[8], 71), 0),
    }


def reference(query_proj, key_proj, value_proj, attn_output, out_grad, log_norm, router_logit, keep_positions):
    scale = HEAD_DIM ** -0.5
    valid = keep_positions >= 0
    gate = jax.nn.sigmoid(router_logit)
    slope = gate * (1.0 - gate)
    grad_wide = out_grad.astype(jnp.float32)
    output_wide = attn_output.astype(jnp.float32)
    router_grad = jnp.where(valid, slope * jnp.sum(grad_wide * output_wide, axis=1), jnp.float32(0.0))
    dout = (gate[:, None] * grad_wide).astype(jnp.bfloat16)
    delta = jnp.sum((dout.astype(jnp.float32) * output_wide).reshape(KEPT_SLOTS, HEADS, HEAD_DIM), axis=2)
    allowed = valid[:, None] & valid[None, :] & (keep_positions[None, :] <= keep_positions[:, None])

    def split_heads(array):
        return array.reshape(KEPT_SLOTS, HEADS, HEAD_DIM).transpose(1, 0, 2)

    def one_head(items):
        query, key, value, grad, norm, offset = items
        scores = jnp.dot(query, key.T, preferred_element_type=jnp.float32) * scale
        prob = jnp.where(allowed, jnp.exp(scores - norm[:, None]), jnp.float32(0.0))
        prob_low = prob.astype(jnp.bfloat16)
        value_part = jnp.dot(prob_low.T, grad, preferred_element_type=jnp.float32)
        dprob = jnp.dot(grad, value.T, preferred_element_type=jnp.float32)
        dscore = (prob * (dprob - offset[:, None]) * scale).astype(jnp.bfloat16)
        query_part = jnp.dot(dscore, key, preferred_element_type=jnp.float32)
        key_part = jnp.dot(dscore.T, query, preferred_element_type=jnp.float32)
        return query_part.astype(jnp.bfloat16), key_part.astype(jnp.bfloat16), value_part.astype(jnp.bfloat16)

    query_heads, key_heads, value_heads = lax.map(one_head, (split_heads(query_proj), split_heads(key_proj), split_heads(value_proj), split_heads(dout), log_norm.T, delta.T))

    def join_heads(array):
        return array.transpose(1, 0, 2).reshape(KEPT_SLOTS, WIDTH)

    return join_heads(query_heads), join_heads(key_heads), join_heads(value_heads), router_grad
```

```python
import math

import jax
import jax.numpy as jnp
from jax import lax
from jax.experimental import pallas as pl
from jax.experimental.pallas import tpu as pltpu
from jax.sharding import PartitionSpec as P

MESH = pl.DeviceIdType.MESH
LOG2E = math.log2(math.e)
SLOTS = 192
HEADS = 6
DIM = 128
SHARDS = 32
CUT = 10
REST = SHARDS - CUT
BLOCK = 4
FAR = 1e30
NEVER = 1e9


def column(row):
    top = jnp.broadcast_to(row[:, :128], (128, 128)).T
    rest = jnp.concatenate([row[:, 128:], row[:, 128:]], axis=1)
    low = jnp.broadcast_to(rest, (128, 128)).T
    return jnp.concatenate([top, low[:64]], axis=0)


def kernel(
    q_hbm, k_hbm, v_hbm, o_ref, g_ref, ln_ref, logit_ref, pos_ref,
    dq_out, dk_out, dv_out, rg_out,
    dout, stat, rbuf, kbuf, vbuf, qbuf, gbuf, sbuf, rowid, dkacc, dvacc, dqacc,
    dksend, dvsend, dqsend, dkrecv, dvrecv, dqrecv,
    kv_ssem, q_ssem, kv_rsem, q_rsem, dkv_ssem, dq_ssem, dkv_rsem, dq_rsem, r_ssem, r_rsem,
):
    me = lax.axis_index("seq")
    tp = lax.axis_index("tp")
    z, y, c = me // 8, (me // 2) % 4, me % 2

    barrier = pltpu.get_barrier_semaphore()

    def greet(i, _):
        pl.semaphore_signal(barrier, inc=1, device_id=((me + i) % SHARDS, tp), device_id_type=MESH)
        return 0

    lax.fori_loop(1, SHARDS, greet, 0)
    for i in range(1, 4):
        pl.semaphore_signal(barrier, inc=1, device_id=(me, (tp + i) % 4), device_id_type=MESH)

    logit = logit_ref[...]
    gate = 1.0 / (1.0 + jnp.exp(-logit))
    valid = pos_ref[pl.ds(me, 1), :] >= 0
    gate_col = column(gate)
    lane = lax.broadcasted_iota(jnp.int32, (SLOTS, DIM), 1)
    norms = ln_ref[...]
    table = jnp.zeros((SLOTS, DIM), jnp.float32)
    total = jnp.zeros((SLOTS, 1), jnp.float32)
    for h in range(HEADS):
        grad = g_ref[:, h * DIM : (h + 1) * DIM].astype(jnp.float32)
        wide = o_ref[:, h * DIM : (h + 1) * DIM].astype(jnp.float32)
        low = (gate_col * grad).astype(jnp.bfloat16)
        dout[h] = low
        delta = jnp.sum(low.astype(jnp.float32) * wide, axis=1, keepdims=True)
        total += jnp.sum(grad * wide, axis=1, keepdims=True)
        table = jnp.where(lane == 8 * h, norms[:, h : h + 1] * LOG2E, table)
        table = jnp.where(lane == 8 * h + 1, delta, table)
    table = jnp.where(lane == 8 * HEADS, total, table)
    flat = jnp.concatenate([table, jnp.zeros((64, DIM), jnp.float32)], axis=0).T
    which = lax.broadcasted_iota(jnp.int32, (DIM, 256), 0)
    good = jnp.concatenate(
        [valid.astype(jnp.float32), jnp.zeros((1, 64), jnp.float32)], axis=1
    )
    is_norm = (which % 8 == 0) & (which < 8 * HEADS)
    flat = jnp.where(is_norm & (good < 0.5), FAR, flat)
    stat[...] = flat[: 8 * HEADS + 8]
    rbuf[tp] = stat[pl.ds(8 * HEADS, 8), :]

    pl.semaphore_wait(barrier, SHARDS - 1 + 3)

    def remote(src, dst, ssem, rsem, to):
        return pltpu.make_async_remote_copy(
            src_ref=src, dst_ref=dst, send_sem=ssem, recv_sem=rsem,
            device_id=(to, tp), device_id_type=MESH,
        )

    def push(src, dst, ssem, rsem, to):
        @pl.when(to == me)
        def _():
            pltpu.make_async_copy(src, dst, rsem).start()

        @pl.when(to != me)
        def _():
            remote(src, dst, ssem, rsem, to).start()

    def drain(src, dst, ssem, rsem, to):
        @pl.when(to != me)
        def _():
            remote(src, dst, ssem, rsem, to).wait_send()

    def arrived(dst, rsem):
        remote(dst, dst, dq_ssem.at[0], rsem, (me + 1) % SHARDS).wait_recv()

    def chip_of(role, h):
        a = role * HEADS + h
        cz = a // 3
        return cz * 8 + ((cz + 1 + a % 3) % 4) * 2

    key_role = (me >= CUT).astype(jnp.int32)
    key_slot = me - CUT * key_role
    query_slot = me // 2

    def lanes(ref, h):
        return ref.at[:, pl.ds(pl.multiple_of(h * DIM, DIM), DIM)]

    def key_copies(h, act):
        chip = chip_of(key_role, h)
        for core in range(2):
            act(lanes(k_hbm, h), kbuf.at[key_slot], kv_ssem.at[h, core, 0], kv_rsem.at[key_slot, 0], chip + core)
            act(lanes(v_hbm, h), vbuf.at[key_slot], kv_ssem.at[h, core, 1], kv_rsem.at[key_slot, 1], chip + core)

    def query_copies(h, role, act):
        to = chip_of(role, h) + c
        act(lanes(q_hbm, h), qbuf.at[query_slot], q_ssem.at[h, role, 0], q_rsem.at[query_slot, 0], to)
        act(dout.at[h], gbuf.at[query_slot], q_ssem.at[h, role, 1], q_rsem.at[query_slot, 1], to)
        act(
            stat.at[pl.ds(pl.multiple_of(h * 8, 8), 8), :], sbuf.at[query_slot],
            q_ssem.at[h, role, 2], q_rsem.at[query_slot, 2], to,
        )

    def outgoing(act):
        def keys(h, _):
            key_copies(h, act)
            return 0

        def queries(h, _):
            query_copies(h, 0, act)

            @pl.when(me >= 8)
            def _():
                query_copies(h, 1, act)

            return 0

        lax.fori_loop(0, HEADS, keys, 0)
        lax.fori_loop(0, HEADS, queries, 0)

    outgoing(push)

    def router_copy(i):
        return pltpu.make_async_remote_copy(
            src_ref=stat.at[pl.ds(8 * HEADS, 8), :], dst_ref=rbuf.at[tp],
            send_sem=r_ssem.at[i], recv_sem=r_rsem.at[tp],
            device_id=(me, (tp + i) % 4), device_id_type=MESH,
        )

    for i in range(1, 4):
        router_copy(i).start()

    place = z * 3 + (y - z + 3) % 4
    role = place // HEADS
    head = place % HEADS
    first_key = role * CUT
    n_chunks = jnp.where(role == 0, CUT // 2, REST // 2)

    def chunks_at(b):
        return jnp.where(role == 0, jnp.minimum(4 * b + 4, CUT // 2), jnp.maximum(4 * b - 1, 0))

    def result_copies(kc, act):
        for half in range(2):
            slot = 2 * kc + half
            act(dksend.at[slot], dkrecv.at[head, c], dkv_ssem.at[slot, 0], dkv_rsem.at[head, c, 0], first_key + slot)
            act(dvsend.at[slot], dvrecv.at[head, c], dkv_ssem.at[slot, 1], dkv_rsem.at[head, c, 1], first_key + slot)

    def grad_copy(i, act):
        act(dqsend.at[i], dqrecv.at[head, role], dq_ssem.at[i], dq_rsem.at[head, role], 2 * i + c)

    scale = DIM ** -0.5

    @pl.when(y != z)
    def _():
        def make_ids(i, _):
            shard = first_key + i
            row = lax.broadcasted_iota(jnp.int32, (1, SLOTS), 1) + shard * SLOTS
            row = jnp.where(pos_ref[pl.ds(shard, 1), :] >= 0, row.astype(jnp.float32), NEVER)
            rowid[i] = column(row)
            return 0

        lax.fori_loop(0, 2 * n_chunks, make_ids, 0)

        def clear(i, _):
            dkacc[i] = jnp.zeros((2 * SLOTS, DIM), jnp.float32)
            dvacc[i] = jnp.zeros((2 * SLOTS, DIM), jnp.float32)
            return 0

        lax.fori_loop(0, n_chunks, clear, 0)

        def query_block(b, _):
            def wait_query(i, _):
                arrived(qbuf.at[i], q_rsem.at[i, 0])
                arrived(gbuf.at[i], q_rsem.at[i, 1])
                arrived(sbuf.at[i], q_rsem.at[i, 2])
                return 0

            lax.fori_loop(BLOCK * b, BLOCK * b + BLOCK, wait_query, 0)

            def wait_key(i, _):
                arrived(kbuf.at[i], kv_rsem.at[i, 0])
                arrived(vbuf.at[i], kv_rsem.at[i, 1])
                return 0

            before = jnp.where(b == role, 0, chunks_at(b - 1))
            count = chunks_at(b)
            lax.fori_loop(2 * before, 2 * count, wait_key, 0)

            first = pl.ds(BLOCK * b, BLOCK)
            stats = [sbuf[BLOCK * b + j] for j in range(BLOCK)]
            norm_row = jnp.concatenate([s[0:1, :SLOTS] for s in stats], axis=1)
            delta_row = jnp.concatenate([s[1:2, :SLOTS] for s in stats], axis=1)
            step = lax.broadcasted_iota(jnp.int32, (1, SLOTS), 1)
            col_row = jnp.concatenate(
                [(step + (2 * (BLOCK * b + j) + c) * SLOTS).astype(jnp.float32) for j in range(BLOCK)], axis=1
            )
            dqacc[...] = jnp.zeros_like(dqacc)

            def chunk(kc, _):
                two = pl.ds(2 * kc, 2)
                query = qbuf[first].reshape(BLOCK * SLOTS, DIM)
                grad = gbuf[first].reshape(BLOCK * SLOTS, DIM)
                key = kbuf[two].reshape(2 * SLOTS, DIM)
                value = vbuf[two].reshape(2 * SLOTS, DIM)
                ids = rowid[two].reshape(2 * SLOTS, DIM)
                nt = (((1,), (1,)), ((), ()))
                tn = (((0,), (0,)), ((), ()))
                score = lax.dot_general(key, query, nt, preferred_element_type=jnp.float32)
                score = score * (scale * LOG2E) - norm_row
                ids = jnp.concatenate([ids] * (BLOCK * SLOTS // DIM), axis=1)
                prob = jnp.exp2(jnp.where(ids <= col_row, score, -FAR))
                dprob = lax.dot_general(value, grad, nt, preferred_element_type=jnp.float32)
                dscore = (prob * (dprob - delta_row)).astype(jnp.bfloat16)
                prob_low = prob.astype(jnp.bfloat16)
                dvacc[kc] += jnp.dot(prob_low, grad, preferred_element_type=jnp.float32)
                dkacc[kc] += jnp.dot(dscore, query, preferred_element_type=jnp.float32)
                dqacc[...] += lax.dot_general(key, dscore, tn, preferred_element_type=jnp.float32)

                @pl.when(b == SHARDS // (2 * BLOCK) - 1)
                def _():
                    dksend[two] = (dkacc[kc] * scale).astype(jnp.bfloat16).reshape(2, SLOTS, DIM)
                    dvsend[two] = dvacc[kc].astype(jnp.bfloat16).reshape(2, SLOTS, DIM)
                    result_copies(kc, push)

                return 0

            lax.fori_loop(0, count, chunk, 0)
            dqsend[first] = (dqacc[...].T * scale).astype(jnp.bfloat16).reshape(BLOCK, SLOTS, DIM)

            def give(i, _):
                grad_copy(i, push)
                return 0

            lax.fori_loop(BLOCK * b, BLOCK * b + BLOCK, give, 0)
            return 0

        lax.fori_loop(role, SHARDS // (2 * BLOCK), query_block, 0)

    for i in range(1, 4):
        from_tp = (tp + i) % 4
        arrived(rbuf.at[from_tp], r_rsem.at[from_tp])
    dots = rbuf[0, 0:1, :SLOTS] + rbuf[1, 0:1, :SLOTS] + rbuf[2, 0:1, :SLOTS] + rbuf[3, 0:1, :SLOTS]
    rg_out[...] = jnp.where(valid, gate * (1.0 - gate) * dots, 0.0)

    def add_up(h, _):
        cols = pl.ds(pl.multiple_of(h * DIM, DIM), DIM)
        arrived(dqrecv.at[h, 0], dq_rsem.at[h, 0])

        @pl.when(me >= 8)
        def _():
            arrived(dqrecv.at[h, 1], dq_rsem.at[h, 1])
            both = dqrecv[h, 0].astype(jnp.float32) + dqrecv[h, 1].astype(jnp.float32)
            dq_out[:, cols] = both.astype(jnp.bfloat16)

        @pl.when(me < 8)
        def _():
            dq_out[:, cols] = dqrecv[h, 0]

        for core in range(2):
            arrived(dkrecv.at[h, core], dkv_rsem.at[h, core, 0])
            arrived(dvrecv.at[h, core], dkv_rsem.at[h, core, 1])
        both = dkrecv[h, 0].astype(jnp.float32) + dkrecv[h, 1].astype(jnp.float32)
        dk_out[:, cols] = both.astype(jnp.bfloat16)
        both = dvrecv[h, 0].astype(jnp.float32) + dvrecv[h, 1].astype(jnp.float32)
        dv_out[:, cols] = both.astype(jnp.bfloat16)
        return 0

    lax.fori_loop(0, HEADS, add_up, 0)

    outgoing(drain)
    for i in range(1, 4):
        router_copy(i).wait_send()

    @pl.when(y != z)
    def _():
        def end_results(kc, _):
            result_copies(kc, drain)
            return 0

        def end_grads(i, _):
            grad_copy(i, drain)
            return 0

        lax.fori_loop(0, n_chunks, end_results, 0)
        lax.fori_loop(BLOCK * role, SHARDS // 2, end_grads, 0)


def body(q, k, v, o, g, norm, logit, positions):
    low, wide = jnp.bfloat16, jnp.float32
    whole = pl.BlockSpec(memory_space=pltpu.VMEM)
    far = pl.BlockSpec(memory_space=pl.ANY)
    dma = pltpu.SemaphoreType.DMA
    tile = (SLOTS, DIM)
    out = jax.ShapeDtypeStruct((SLOTS, HEADS * DIM), low)
    dq, dk, dv, router = pl.pallas_call(
        kernel,
        out_shape=(out, out, out, jax.ShapeDtypeStruct((1, SLOTS), wide)),
        in_specs=[far, far, far, whole, whole, whole, whole, whole],
        out_specs=(whole, whole, whole, whole),
        scratch_shapes=[
            pltpu.VMEM((HEADS,) + tile, low),
            pltpu.VMEM((8 * HEADS + 8, 256), wide),
            pltpu.VMEM((4, 8, 256), wide),
            pltpu.VMEM((REST,) + tile, low),
            pltpu.VMEM((REST,) + tile, low),
            pltpu.VMEM((16,) + tile, low),
            pltpu.VMEM((16,) + tile, low),
            pltpu.VMEM((16, 8, 256), wide),
            pltpu.VMEM((REST,) + tile, wide),
            pltpu.VMEM((REST // 2, 2 * SLOTS, DIM), wide),
            pltpu.VMEM((REST // 2, 2 * SLOTS, DIM), wide),
            pltpu.VMEM((DIM, BLOCK * SLOTS), wide),
            pltpu.VMEM((REST,) + tile, low),
            pltpu.VMEM((REST,) + tile, low),
            pltpu.VMEM((16,) + tile, low),
            pltpu.VMEM((HEADS, 2) + tile, low),
            pltpu.VMEM((HEADS, 2) + tile, low),
            pltpu.VMEM((HEADS, 2) + tile, low),
            dma((HEADS, 2, 2)),
            dma((HEADS, 2, 3)),
            dma((REST, 2)),
            dma((16, 3)),
            dma((REST, 2)),
            dma((16,)),
            dma((HEADS, 2, 2)),
            dma((HEADS, 2)),
            dma((4,)),
            dma((4,)),
        ],
        compiler_params=pltpu.CompilerParams(
            collective_id=0, has_side_effects=True, vmem_limit_bytes=56 * 2**20
        ),
        cost_estimate=pl.CostEstimate(flops=9_000_000_000, bytes_accessed=4_000_000, transcendentals=6_000_000),
    )(q, k, v, o, g, norm, logit.reshape(1, SLOTS), positions.reshape(SHARDS, SLOTS))
    return dq, dk, dv, router.reshape(SLOTS)


def solution(mesh):
    split = P("seq", "tp")
    return jax.shard_map(
        body,
        mesh=mesh,
        in_specs=(split, split, split, split, split, split, P("seq"), P()),
        out_specs=(split, split, split, P("seq")),
        check_vma=False,
    )
```

```python
import math

import jax
import jax.numpy as jnp
from jax import lax
from jax.experimental import pallas as pl
from jax.experimental.pallas import tpu as pltpu
from jax.sharding import PartitionSpec as P

MESH = pl.DeviceIdType.MESH
LOG2E = math.log2(math.e)
SLOTS = 192
HEADS = 6
DIM = 128
SHARDS = 32
CUT = 12
REST = SHARDS - CUT
BLOCK = 4
FAR = 1e30
NEVER = 1e9


def column(row):
    top = jnp.broadcast_to(row[:, :128], (128, 128)).T
    rest = jnp.concatenate([row[:, 128:], row[:, 128:]], axis=1)
    low = jnp.broadcast_to(rest, (128, 128)).T
    return jnp.concatenate([top, low[:64]], axis=0)


def kernel(
    q_hbm, k_hbm, v_hbm, o_ref, g_ref, ln_ref, logit_ref, pos_ref,
    dqa_out, dqb_out, dk_out, dv_out, rg_out,
    dout, stat, rbuf, kbuf, vbuf, qbuf, gbuf, sbuf, rowid, dkacc, dvacc, dqacc,
    xsend, xrecv, dkvsend, dqsend,
    kv_ssem, q_ssem, kv_rsem, q_rsem, fwd_ssem, x_ssem, x_rsem, dkv_ssem, dq_ssem, dkv_rsem, dq_rsem, r_ssem, r_rsem,
):
    me = lax.axis_index("seq")
    tp = lax.axis_index("tp")
    z, y, c = me // 8, (me // 2) % 4, me % 2
    sibling = me + 1 - 2 * c

    barrier = pltpu.get_barrier_semaphore()

    def greet(i, _):
        pl.semaphore_signal(barrier, inc=1, device_id=((me + i) % SHARDS, tp), device_id_type=MESH)
        return 0

    lax.fori_loop(1, SHARDS, greet, 0)
    for i in range(1, 4):
        pl.semaphore_signal(barrier, inc=1, device_id=(me, (tp + i) % 4), device_id_type=MESH)

    logit = logit_ref[...]
    gate = 1.0 / (1.0 + jnp.exp(-logit))
    at = (me * 3) // 2
    top, low = pos_ref[pl.ds(at, 1), :], pos_ref[pl.ds(at + 1, 1), :]
    even = jnp.concatenate([top, low[:, :64]], axis=1)
    odd = jnp.concatenate([top[:, 64:], low], axis=1)
    valid = jnp.where(c == 0, even, odd) >= 0
    gate_col = column(gate)
    lane = lax.broadcasted_iota(jnp.int32, (SLOTS, DIM), 1)
    table = jnp.zeros((SLOTS, DIM), jnp.float32)
    total = jnp.zeros((SLOTS, 1), jnp.float32)
    for h in range(HEADS):
        grad = g_ref[:, h * DIM : (h + 1) * DIM].astype(jnp.float32)
        wide = o_ref[:, h * DIM : (h + 1) * DIM].astype(jnp.float32)
        low = (gate_col * grad).astype(jnp.bfloat16)
        dout[h] = low
        delta = jnp.sum(low.astype(jnp.float32) * wide, axis=1, keepdims=True)
        total += jnp.sum(grad * wide, axis=1, keepdims=True)
        table = jnp.where(lane == 8 * h + 1, delta, table)
    table = jnp.where(lane == 8 * HEADS, total, table)
    flat = jnp.concatenate([table, jnp.zeros((64, DIM), jnp.float32)], axis=0).T
    stat[...] = flat[: 8 * HEADS + 8]
    for h in range(HEADS):
        norm = jnp.where(valid, ln_ref[h : h + 1, :] * LOG2E, FAR)
        stat[8 * h : 8 * h + 1, :SLOTS] = norm
    rbuf[tp] = stat[pl.ds(8 * HEADS, 8), :]

    place = z * 3 + (y - z + 3) % 4
    role = place // HEADS
    head = place % HEADS
    first_key = role * CUT
    n_chunks = jnp.where(role == 0, CUT // 2, REST // 2)

    def chunks_at(b):
        return jnp.where(role == 0, jnp.minimum(4 * b + 4, CUT // 2), jnp.maximum(4 * b - 2, 0))

    @pl.when(y != z)
    def _():
        def make_ids(i, _):
            for j in range(3):
                at = (first_key * 3) // 2 + 3 * i + j
                row = lax.broadcasted_iota(jnp.int32, (1, DIM), 1) + at * DIM
                row = jnp.where(pos_ref[pl.ds(at, 1), :] >= 0, row.astype(jnp.float32), NEVER)
                rowid[i, DIM * j : DIM * (j + 1), :] = jnp.broadcast_to(row, (DIM, DIM)).T
            dkacc[i] = jnp.zeros((2 * SLOTS, DIM), jnp.float32)
            dvacc[i] = jnp.zeros((2 * SLOTS, DIM), jnp.float32)
            return 0

        lax.fori_loop(0, n_chunks, make_ids, 0)

        @pl.when(role == 1)
        def _():
            for i in (CUT // 2 - 2, CUT // 2 - 1):
                qbuf[i] = jnp.zeros((SLOTS, DIM), jnp.bfloat16)
                gbuf[i] = jnp.zeros((SLOTS, DIM), jnp.bfloat16)
                sbuf[i] = jnp.zeros((8, 256), jnp.float32)

    pl.semaphore_wait(barrier, SHARDS - 1 + 3)

    def remote(src, dst, ssem, rsem, to):
        return pltpu.make_async_remote_copy(
            src_ref=src, dst_ref=dst, send_sem=ssem, recv_sem=rsem,
            device_id=(to, tp), device_id_type=MESH,
        )

    def push(src, dst, ssem, rsem, to):
        @pl.when(to == me)
        def _():
            pltpu.make_async_copy(src, dst, rsem).start()

        @pl.when(to != me)
        def _():
            remote(src, dst, ssem, rsem, to).start()

    def drain(src, dst, ssem, rsem, to):
        @pl.when(to != me)
        def _():
            remote(src, dst, ssem, rsem, to).wait_send()

    def arrived(dst, rsem):
        remote(dst, dst, dq_ssem.at[0], rsem, (me + 1) % SHARDS).wait_recv()

    def chip_of(role, h):
        a = role * HEADS + h
        cz = a // 3
        return cz * 8 + ((cz + 1 + a % 3) % 4) * 2

    key_role = (me >= CUT).astype(jnp.int32)
    key_slot = me - CUT * key_role
    query_slot = me // 2

    def lanes(ref, h):
        return ref.at[:, pl.ds(pl.multiple_of(h * DIM, DIM), DIM)]

    def key_copies(h, act):
        to = chip_of(key_role, h) + c
        act(lanes(k_hbm, h), kbuf.at[key_slot], kv_ssem.at[h, 0], kv_rsem.at[key_slot, 0], to)
        act(lanes(v_hbm, h), vbuf.at[key_slot], kv_ssem.at[h, 1], kv_rsem.at[key_slot, 1], to)

    def query_copies(h, role, act):
        to = chip_of(role, h) + c
        act(lanes(q_hbm, h), qbuf.at[query_slot], q_ssem.at[h, role, 0], q_rsem.at[query_slot, 0], to)
        act(dout.at[h], gbuf.at[query_slot], q_ssem.at[h, role, 1], q_rsem.at[query_slot, 1], to)
        act(
            stat.at[pl.ds(pl.multiple_of(h * 8, 8), 8), :], sbuf.at[query_slot],
            q_ssem.at[h, role, 2], q_rsem.at[query_slot, 2], to,
        )

    def outgoing(act):
        chip = me // 2

        def keys(i, _):
            key_copies((chip + i) % HEADS, act)
            return 0

        def queries(i, _):
            target = ((chip * 3) // 4 + i) % (2 * HEADS)

            @pl.when((target < HEADS) | (me >= CUT))
            def _():
                query_copies(target % HEADS, target // HEADS, act)

            return 0

        lax.fori_loop(0, HEADS, keys, 0)
        lax.fori_loop(0, 2 * HEADS, queries, 0)

    outgoing(push)

    def router_copy(i):
        return pltpu.make_async_remote_copy(
            src_ref=stat.at[pl.ds(8 * HEADS, 8), :], dst_ref=rbuf.at[tp],
            send_sem=r_ssem.at[i], recv_sem=r_rsem.at[tp],
            device_id=(me, (tp + i) % 4), device_id_type=MESH,
        )

    for i in range(1, 4):
        router_copy(i).start()

    def forward_copies(kc, act):
        slot = 2 * kc + c
        act(kbuf.at[slot], kbuf.at[slot], fwd_ssem.at[kc, 0], kv_rsem.at[slot, 0], sibling)
        act(vbuf.at[slot], vbuf.at[slot], fwd_ssem.at[kc, 1], kv_rsem.at[slot, 1], sibling)

    def exchange_copy(kc, act):
        act(xsend.at[kc], xrecv.at[kc], x_ssem.at[kc], x_rsem.at[kc], sibling)

    def result_copies(kc, act):
        owner = first_key + 2 * kc + c
        act(dkvsend.at[kc, 0], lanes(dk_out, head), dkv_ssem.at[kc, 0], dkv_rsem.at[head, 0], owner)
        act(dkvsend.at[kc, 1], lanes(dv_out, head), dkv_ssem.at[kc, 1], dkv_rsem.at[head, 1], owner)

    def grad_copy(i, act):
        @pl.when(role == 0)
        def _():
            act(dqsend.at[i], lanes(dqa_out, head), dq_ssem.at[i], dq_rsem.at[head, 0], 2 * i + c)

        @pl.when(role == 1)
        def _():
            act(dqsend.at[i], lanes(dqb_out, head), dq_ssem.at[i], dq_rsem.at[head, 1], 2 * i + c)

    scale = DIM ** -0.5
    last = SHARDS // (2 * BLOCK) - 1
    first_query = role * (CUT // 2)

    @pl.when(y != z)
    def _():
        def query_block(b, _):
            def wait_query(i, _):
                arrived(qbuf.at[i], q_rsem.at[i, 0])
                arrived(gbuf.at[i], q_rsem.at[i, 1])
                arrived(sbuf.at[i], q_rsem.at[i, 2])
                return 0

            def own_key(kc, _):
                slot = 2 * kc + c
                arrived(kbuf.at[slot], kv_rsem.at[slot, 0])
                arrived(vbuf.at[slot], kv_rsem.at[slot, 1])
                forward_copies(kc, push)
                return 0

            def other_key(kc, _):
                slot = 2 * kc + 1 - c
                arrived(kbuf.at[slot], kv_rsem.at[slot, 0])
                arrived(vbuf.at[slot], kv_rsem.at[slot, 1])
                return 0

            before = jnp.where(b == role, 0, chunks_at(b - 1))
            count = chunks_at(b)
            start = jnp.maximum(BLOCK * b, first_query)
            lax.fori_loop(before, count, own_key, 0)
            lax.fori_loop(start, BLOCK * b + BLOCK, wait_query, 0)
            lax.fori_loop(before, count, other_key, 0)

            first = pl.ds(BLOCK * b, BLOCK)
            stats = [sbuf[BLOCK * b + j] for j in range(BLOCK)]
            norm_row = jnp.concatenate([s[0:1, :SLOTS] for s in stats], axis=1)
            delta_row = jnp.concatenate([s[1:2, :SLOTS] for s in stats], axis=1)
            step = lax.broadcasted_iota(jnp.int32, (1, SLOTS), 1)
            col_row = jnp.concatenate(
                [(step + (2 * (BLOCK * b + j) + c) * SLOTS).astype(jnp.float32) for j in range(BLOCK)], axis=1
            )
            dqacc[...] = jnp.zeros_like(dqacc)

            def turn(i):
                return (i + (head * count) // HEADS) % count

            def finish(kc):
                mine = pl.ds(pl.multiple_of(c * SLOTS, SLOTS), SLOTS)
                arrived(xrecv.at[kc], x_rsem.at[kc])
                both = dkacc[kc, mine, :] * scale + xrecv[kc, 0].astype(jnp.float32)
                dkvsend[kc, 0] = both.astype(jnp.bfloat16)
                both = dvacc[kc, mine, :] + xrecv[kc, 1].astype(jnp.float32)
                dkvsend[kc, 1] = both.astype(jnp.bfloat16)
                result_copies(kc, push)

            def chunk(i, _):
                kc = turn(i)
                two = pl.ds(2 * kc, 2)
                query = qbuf[first].reshape(BLOCK * SLOTS, DIM)
                grad = gbuf[first].reshape(BLOCK * SLOTS, DIM)
                key = kbuf[two].reshape(2 * SLOTS, DIM)
                value = vbuf[two].reshape(2 * SLOTS, DIM)
                ids = rowid[kc]
                nt = (((1,), (1,)), ((), ()))
                tn = (((0,), (0,)), ((), ()))
                score = lax.dot_general(key, query, nt, preferred_element_type=jnp.float32)
                score = score * (scale * LOG2E) - norm_row
                ids = jnp.concatenate([ids] * (BLOCK * SLOTS // DIM), axis=1)
                prob = jnp.exp2(jnp.where(ids <= col_row, score, -FAR))
                dprob = lax.dot_general(value, grad, nt, preferred_element_type=jnp.float32)
                dscore = (prob * (dprob - delta_row)).astype(jnp.bfloat16)
                prob_low = prob.astype(jnp.bfloat16)
                dvacc[kc] += jnp.dot(prob_low, grad, preferred_element_type=jnp.float32)
                dkacc[kc] += jnp.dot(dscore, query, preferred_element_type=jnp.float32)
                dqacc[...] += lax.dot_general(key, dscore, tn, preferred_element_type=jnp.float32)

                @pl.when(b == last)
                def _():
                    theirs = pl.ds(pl.multiple_of((1 - c) * SLOTS, SLOTS), SLOTS)
                    xsend[kc, 0] = (dkacc[kc, theirs, :] * scale).astype(jnp.bfloat16)
                    xsend[kc, 1] = dvacc[kc, theirs, :].astype(jnp.bfloat16)
                    exchange_copy(kc, push)

                    @pl.when(i > 0)
                    def _():
                        finish(turn(i - 1))

                return 0

            lax.fori_loop(0, count, chunk, 0)

            @pl.when(b == last)
            def _():
                finish(turn(count - 1))

            dqsend[first] = (dqacc[...].T * scale).astype(jnp.bfloat16).reshape(BLOCK, SLOTS, DIM)

            def give(i, _):
                grad_copy(i, push)
                return 0

            lax.fori_loop(start, BLOCK * b + BLOCK, give, 0)
            return 0

        lax.fori_loop(role, last + 1, query_block, 0)

    for i in range(1, 4):
        from_tp = (tp + i) % 4
        arrived(rbuf.at[from_tp], r_rsem.at[from_tp])
    dots = rbuf[0, 0:1, :SLOTS] + rbuf[1, 0:1, :SLOTS] + rbuf[2, 0:1, :SLOTS] + rbuf[3, 0:1, :SLOTS]
    rg_out[...] = jnp.where(valid, gate * (1.0 - gate) * dots, 0.0)

    def collect(h, _):
        arrived(lanes(dqa_out, h), dq_rsem.at[h, 0])

        @pl.when(me >= CUT)
        def _():
            arrived(lanes(dqb_out, h), dq_rsem.at[h, 1])

        arrived(lanes(dk_out, h), dkv_rsem.at[h, 0])
        arrived(lanes(dv_out, h), dkv_rsem.at[h, 1])
        return 0

    lax.fori_loop(0, HEADS, collect, 0)

    outgoing(drain)
    for i in range(1, 4):
        router_copy(i).wait_send()

    @pl.when(y != z)
    def _():
        def end_results(kc, _):
            forward_copies(kc, drain)
            exchange_copy(kc, drain)
            result_copies(kc, drain)
            return 0

        def end_grads(i, _):
            grad_copy(i, drain)
            return 0

        lax.fori_loop(0, n_chunks, end_results, 0)
        lax.fori_loop(first_query, SHARDS // 2, end_grads, 0)


def finish_kernel(dqa, dqb, dk, dv, router, dq_out, dk_out, dv_out, rg_out, buf, in_sems, out_sems):
    me = lax.axis_index("seq")
    parts = [pltpu.make_async_copy(ref, buf.at[i], in_sems.at[i]) for i, ref in enumerate((dk, dv, dqa, dqb))]
    results = [
        pltpu.make_async_copy(buf.at[i], ref, out_sems.at[i]) for i, ref in enumerate((dk_out, dv_out, dq_out))
    ]
    for i in range(3):
        parts[i].start()

    @pl.when(me >= CUT)
    def _():
        parts[3].start()

    rg_out[...] = router[...]
    for i in range(2):
        parts[i].wait()
        results[i].start()
    parts[2].wait()

    @pl.when(me >= CUT)
    def _():
        parts[3].wait()
        buf[2] = (buf[2].astype(jnp.float32) + buf[3].astype(jnp.float32)).astype(jnp.bfloat16)

    results[2].start()
    for result in results:
        result.wait()


def body(q, k, v, o, g, norm, logit, positions):
    low, wide = jnp.bfloat16, jnp.float32
    whole = pl.BlockSpec(memory_space=pltpu.VMEM)
    far = pl.BlockSpec(memory_space=pl.ANY)
    dma = pltpu.SemaphoreType.DMA
    tile = (SLOTS, DIM)
    half = REST // 2
    out = jax.ShapeDtypeStruct((SLOTS, HEADS * DIM), low)
    row = jax.ShapeDtypeStruct((1, SLOTS), wide)
    dqa, dqb, dk, dv, router = pl.pallas_call(
        kernel,
        out_shape=(out, out, out, out, row),
        in_specs=[far, far, far, whole, whole, whole, whole, whole],
        out_specs=(far, far, far, far, whole),
        scratch_shapes=[
            pltpu.VMEM((HEADS,) + tile, low),
            pltpu.VMEM((8 * HEADS + 8, 256), wide),
            pltpu.VMEM((4, 8, 256), wide),
            pltpu.VMEM((REST,) + tile, low),
            pltpu.VMEM((REST,) + tile, low),
            pltpu.VMEM((16,) + tile, low),
            pltpu.VMEM((16,) + tile, low),
            pltpu.VMEM((16, 8, 256), wide),
            pltpu.VMEM((half, 2 * SLOTS, DIM), wide),
            pltpu.VMEM((half, 2 * SLOTS, DIM), wide),
            pltpu.VMEM((half, 2 * SLOTS, DIM), wide),
            pltpu.VMEM((DIM, BLOCK * SLOTS), wide),
            pltpu.VMEM((half, 2) + tile, low),
            pltpu.VMEM((half, 2) + tile, low),
            pltpu.VMEM((half, 2) + tile, low),
            pltpu.VMEM((16,) + tile, low),
            dma((HEADS, 2)),
            dma((HEADS, 2, 3)),
            dma((REST, 2)),
            dma((16, 3)),
            dma((half, 2)),
            dma((half,)),
            dma((half,)),
            dma((half, 2)),
            dma((16,)),
            dma((HEADS, 2)),
            dma((HEADS, 2)),
            dma((4,)),
            dma((4,)),
        ],
        compiler_params=pltpu.CompilerParams(
            collective_id=0, has_side_effects=True, vmem_limit_bytes=56 * 2**20
        ),
        cost_estimate=pl.CostEstimate(flops=9_000_000_000, bytes_accessed=4_000_000, transcendentals=6_000_000),
    )(q, k, v, o, g, norm.T, logit.reshape(1, SLOTS), positions.reshape(-1, DIM))
    dq, dk, dv, router = pl.pallas_call(
        finish_kernel,
        out_shape=(out, out, out, row),
        in_specs=[far, far, far, far, whole],
        out_specs=(far, far, far, whole),
        scratch_shapes=[
            pltpu.VMEM((4, SLOTS, HEADS * DIM), low),
            dma((4,)),
            dma((3,)),
        ],
        compiler_params=pltpu.CompilerParams(vmem_limit_bytes=56 * 2**20),
    )(dqa, dqb, dk, dv, router)
    return dq, dk, dv, router.reshape(SLOTS)


def solution(mesh):
    split = P("seq", "tp")
    return jax.shard_map(
        body,
        mesh=mesh,
        in_specs=(split, split, split, split, split, split, P("seq"), P()),
        out_specs=(split, split, split, P("seq")),
        check_vma=False,
    )
```

```python
import math

import jax
import jax.numpy as jnp
from jax import lax
from jax.experimental import pallas as pl
from jax.experimental.pallas import tpu as pltpu
from jax.sharding import PartitionSpec as P

MESH = pl.DeviceIdType.MESH
LOG2E = math.log2(math.e)
SLOTS = 192
HEADS = 6
DIM = 128
SHARDS = 32
CUT = 12
REST = SHARDS - CUT
BLOCK = 4
FAR = 1e30
NEVER = 1e9


def column(row):
    top = jnp.broadcast_to(row[:, :128], (128, 128)).T
    rest = jnp.concatenate([row[:, 128:], row[:, 128:]], axis=1)
    low = jnp.broadcast_to(rest, (128, 128)).T
    return jnp.concatenate([top, low[:64]], axis=0)


def kernel(
    q_hbm, k_hbm, v_hbm, o_ref, g_ref, ln_ref, logit_ref, pos_ref,
    dqa_out, dqb_out, dk_out, dv_out, rg_out,
    dout, stat, rbuf, kbuf, vbuf, qbuf, gbuf, sbuf, rowid, dkacc, dvacc, dqacc,
    xsend, xrecv, dkvsend, dqsend,
    kv_ssem, q_ssem, kv_rsem, q_rsem, fwd_ssem, x_ssem, x_rsem, dkv_ssem, dq_ssem, dkv_rsem, dq_rsem, r_ssem, r_rsem,
):
    me = lax.axis_index("seq")
    tp = lax.axis_index("tp")
    z, y, c = me // 8, (me // 2) % 4, me % 2
    sibling = me + 1 - 2 * c

    barrier = pltpu.get_barrier_semaphore()

    def greet(i, _):
        pl.semaphore_signal(barrier, inc=1, device_id=((me + i) % SHARDS, tp), device_id_type=MESH)
        return 0

    lax.fori_loop(1, SHARDS, greet, 0)
    for i in range(1, 4):
        pl.semaphore_signal(barrier, inc=1, device_id=(me, (tp + i) % 4), device_id_type=MESH)

    logit = logit_ref[...]
    gate = 1.0 / (1.0 + jnp.exp(-logit))
    at = (me * 3) // 2
    top, low = pos_ref[pl.ds(at, 1), :], pos_ref[pl.ds(at + 1, 1), :]
    even = jnp.concatenate([top, low[:, :64]], axis=1)
    odd = jnp.concatenate([top[:, 64:], low], axis=1)
    valid = jnp.where(c == 0, even, odd) >= 0
    gate_col = column(gate)
    lane = lax.broadcasted_iota(jnp.int32, (SLOTS, DIM), 1)
    table = jnp.zeros((SLOTS, DIM), jnp.float32)
    total = jnp.zeros((SLOTS, 1), jnp.float32)
    for h in range(HEADS):
        grad = g_ref[:, h * DIM : (h + 1) * DIM].astype(jnp.float32)
        wide = o_ref[:, h * DIM : (h + 1) * DIM].astype(jnp.float32)
        low = (gate_col * grad).astype(jnp.bfloat16)
        dout[h] = low
        delta = jnp.sum(low.astype(jnp.float32) * wide, axis=1, keepdims=True)
        total += jnp.sum(grad * wide, axis=1, keepdims=True)
        table = jnp.where(lane == 8 * h + 1, delta, table)
    table = jnp.where(lane == 8 * HEADS, total, table)
    flat = jnp.concatenate([table, jnp.zeros((64, DIM), jnp.float32)], axis=0).T
    stat[...] = flat[: 8 * HEADS + 8]
    for h in range(HEADS):
        norm = jnp.where(valid, ln_ref[h : h + 1, :] * LOG2E, FAR)
        stat[8 * h : 8 * h + 1, :SLOTS] = norm
    rbuf[tp] = stat[pl.ds(8 * HEADS, 8), :]

    place = z * 3 + (y - z + 3) % 4
    role = place // HEADS
    head = place % HEADS
    first_key = role * CUT
    n_chunks = jnp.where(role == 0, CUT // 2, REST // 2)

    def chunks_at(b):
        return jnp.where(role == 0, jnp.minimum(4 * b + 4, CUT // 2), jnp.maximum(4 * b - 2, 0))

    @pl.when(y != z)
    def _():
        def make_ids(i, _):
            for j in range(3):
                at = (first_key * 3) // 2 + 3 * i + j
                row = lax.broadcasted_iota(jnp.int32, (1, DIM), 1) + at * DIM
                row = jnp.where(pos_ref[pl.ds(at, 1), :] >= 0, row.astype(jnp.float32), NEVER)
                rowid[i, DIM * j : DIM * (j + 1), :] = jnp.broadcast_to(row, (DIM, DIM)).T
            dkacc[i] = jnp.zeros((2 * SLOTS, DIM), jnp.float32)
            dvacc[i] = jnp.zeros((2 * SLOTS, DIM), jnp.float32)
            return 0

        lax.fori_loop(0, n_chunks, make_ids, 0)

        @pl.when(role == 1)
        def _():
            for i in (CUT // 2 - 2, CUT // 2 - 1):
                qbuf[i] = jnp.zeros((SLOTS, DIM), jnp.bfloat16)
                gbuf[i] = jnp.zeros((SLOTS, DIM), jnp.bfloat16)
                sbuf[i] = jnp.zeros((8, 256), jnp.float32)

    pl.semaphore_wait(barrier, SHARDS - 1 + 3)

    def remote(src, dst, ssem, rsem, to):
        return pltpu.make_async_remote_copy(
            src_ref=src, dst_ref=dst, send_sem=ssem, recv_sem=rsem,
            device_id=(to, tp), device_id_type=MESH,
        )

    def push(src, dst, ssem, rsem, to):
        @pl.when(to == me)
        def _():
            pltpu.make_async_copy(src, dst, rsem).start()

        @pl.when(to != me)
        def _():
            remote(src, dst, ssem, rsem, to).start()

    def drain(src, dst, ssem, rsem, to):
        @pl.when(to != me)
        def _():
            remote(src, dst, ssem, rsem, to).wait_send()

    def arrived(dst, rsem):
        remote(dst, dst, dq_ssem.at[0], rsem, (me + 1) % SHARDS).wait_recv()

    def chip_of(role, h):
        a = role * HEADS + h
        cz = a // 3
        return cz * 8 + ((cz + 1 + a % 3) % 4) * 2

    key_role = (me >= CUT).astype(jnp.int32)
    key_slot = me - CUT * key_role
    query_slot = me // 2

    def lanes(ref, h):
        return ref.at[:, pl.ds(pl.multiple_of(h * DIM, DIM), DIM)]

    def key_copies(h, act):
        to = chip_of(key_role, h) + c
        act(lanes(k_hbm, h), kbuf.at[key_slot], kv_ssem.at[h, 0], kv_rsem.at[key_slot, 0], to)
        act(lanes(v_hbm, h), vbuf.at[key_slot], kv_ssem.at[h, 1], kv_rsem.at[key_slot, 1], to)

    def query_copies(h, role, act):
        to = chip_of(role, h) + c
        act(lanes(q_hbm, h), qbuf.at[query_slot], q_ssem.at[h, role, 0], q_rsem.at[query_slot, 0], to)
        act(dout.at[h], gbuf.at[query_slot], q_ssem.at[h, role, 1], q_rsem.at[query_slot, 1], to)
        act(
            stat.at[pl.ds(pl.multiple_of(h * 8, 8), 8), :], sbuf.at[query_slot],
            q_ssem.at[h, role, 2], q_rsem.at[query_slot, 2], to,
        )

    def outgoing(act):
        chip = me // 2

        def keys(i, _):
            key_copies((chip + i) % HEADS, act)
            return 0

        def queries(i, _):
            target = ((chip * 3) // 4 + i) % (2 * HEADS)

            @pl.when((target < HEADS) | (me >= CUT))
            def _():
                query_copies(target % HEADS, target // HEADS, act)

            return 0

        lax.fori_loop(0, HEADS, keys, 0)
        lax.fori_loop(0, 2 * HEADS, queries, 0)

    outgoing(push)

    def router_copy(i):
        return pltpu.make_async_remote_copy(
            src_ref=stat.at[pl.ds(8 * HEADS, 8), :], dst_ref=rbuf.at[tp],
            send_sem=r_ssem.at[i], recv_sem=r_rsem.at[tp],
            device_id=(me, (tp + i) % 4), device_id_type=MESH,
        )

    for i in range(1, 4):
        router_copy(i).start()

    def forward_copies(kc, act):
        slot = 2 * kc + c
        act(kbuf.at[slot], kbuf.at[slot], fwd_ssem.at[kc, 0], kv_rsem.at[slot, 0], sibling)
        act(vbuf.at[slot], vbuf.at[slot], fwd_ssem.at[kc, 1], kv_rsem.at[slot, 1], sibling)

    def exchange_copy(kc, act):
        act(xsend.at[kc], xrecv.at[kc], x_ssem.at[kc], x_rsem.at[kc], sibling)

    def result_copies(kc, act):
        owner = first_key + 2 * kc + c
        act(dkvsend.at[kc, 0], lanes(dk_out, head), dkv_ssem.at[kc, 0], dkv_rsem.at[head, 0], owner)
        act(dkvsend.at[kc, 1], lanes(dv_out, head), dkv_ssem.at[kc, 1], dkv_rsem.at[head, 1], owner)

    def grad_copy(i, act):
        @pl.when(role == 0)
        def _():
            act(dqsend.at[i], lanes(dqa_out, head), dq_ssem.at[i], dq_rsem.at[head, 0], 2 * i + c)

        @pl.when(role == 1)
        def _():
            act(dqsend.at[i], lanes(dqb_out, head), dq_ssem.at[i], dq_rsem.at[head, 1], 2 * i + c)

    scale = DIM ** -0.5
    last = SHARDS // (2 * BLOCK) - 1
    first_query = role * (CUT // 2)

    @pl.when(y != z)
    def _():
        def own_key(kc, _):
            slot = 2 * kc + c
            arrived(kbuf.at[slot], kv_rsem.at[slot, 0])
            arrived(vbuf.at[slot], kv_rsem.at[slot, 1])
            forward_copies(kc, push)
            return 0

        lax.fori_loop(0, n_chunks, own_key, 0)

        def query_block(b, _):
            def wait_query(i, _):
                arrived(qbuf.at[i], q_rsem.at[i, 0])
                arrived(gbuf.at[i], q_rsem.at[i, 1])
                arrived(sbuf.at[i], q_rsem.at[i, 2])
                return 0

            def other_key(kc, _):
                slot = 2 * kc + 1 - c
                arrived(kbuf.at[slot], kv_rsem.at[slot, 0])
                arrived(vbuf.at[slot], kv_rsem.at[slot, 1])
                return 0

            before = jnp.where(b == role, 0, chunks_at(b - 1))
            count = chunks_at(b)
            start = jnp.maximum(BLOCK * b, first_query)
            lax.fori_loop(start, BLOCK * b + BLOCK, wait_query, 0)
            lax.fori_loop(before, count, other_key, 0)

            first = pl.ds(BLOCK * b, BLOCK)
            stats = [sbuf[BLOCK * b + j] for j in range(BLOCK)]
            norm_row = jnp.concatenate([s[0:1, :SLOTS] for s in stats], axis=1)
            delta_row = jnp.concatenate([s[1:2, :SLOTS] for s in stats], axis=1)
            step = lax.broadcasted_iota(jnp.int32, (1, SLOTS), 1)
            col_row = jnp.concatenate(
                [(step + (2 * (BLOCK * b + j) + c) * SLOTS).astype(jnp.float32) for j in range(BLOCK)], axis=1
            )
            dqacc[...] = jnp.zeros_like(dqacc)

            def turn(i):
                return (i + (head * count) // HEADS) % count

            def finish(kc):
                mine = pl.ds(pl.multiple_of(c * SLOTS, SLOTS), SLOTS)
                arrived(xrecv.at[kc], x_rsem.at[kc])
                both = dkacc[kc, mine, :] * scale + xrecv[kc, 0].astype(jnp.float32)
                dkvsend[kc, 0] = both.astype(jnp.bfloat16)
                both = dvacc[kc, mine, :] + xrecv[kc, 1].astype(jnp.float32)
                dkvsend[kc, 1] = both.astype(jnp.bfloat16)
                result_copies(kc, push)

            def chunk(i, _):
                kc = turn(i)
                two = pl.ds(2 * kc, 2)
                query = qbuf[first].reshape(BLOCK * SLOTS, DIM)
                grad = gbuf[first].reshape(BLOCK * SLOTS, DIM)
                key = kbuf[two].reshape(2 * SLOTS, DIM)
                value = vbuf[two].reshape(2 * SLOTS, DIM)
                ids = rowid[kc]
                nt = (((1,), (1,)), ((), ()))
                tn = (((0,), (0,)), ((), ()))
                score = lax.dot_general(key, query, nt, preferred_element_type=jnp.float32)
                score = score * (scale * LOG2E) - norm_row
                ids = jnp.concatenate([ids] * (BLOCK * SLOTS // DIM), axis=1)
                prob = jnp.exp2(jnp.where(ids <= col_row, score, -FAR))
                dprob = lax.dot_general(value, grad, nt, preferred_element_type=jnp.float32)
                dscore = (prob * (dprob - delta_row)).astype(jnp.bfloat16)
                prob_low = prob.astype(jnp.bfloat16)
                dvacc[kc] += jnp.dot(prob_low, grad, preferred_element_type=jnp.float32)
                dkacc[kc] += jnp.dot(dscore, query, preferred_element_type=jnp.float32)
                dqacc[...] += lax.dot_general(key, dscore, tn, preferred_element_type=jnp.float32)

                @pl.when(b == last)
                def _():
                    theirs = pl.ds(pl.multiple_of((1 - c) * SLOTS, SLOTS), SLOTS)
                    xsend[kc, 0] = (dkacc[kc, theirs, :] * scale).astype(jnp.bfloat16)
                    xsend[kc, 1] = dvacc[kc, theirs, :].astype(jnp.bfloat16)
                    exchange_copy(kc, push)

                    @pl.when(i > 0)
                    def _():
                        finish(turn(i - 1))

                return 0

            lax.fori_loop(0, count, chunk, 0)

            @pl.when(b == last)
            def _():
                finish(turn(count - 1))

            dqsend[first] = (dqacc[...].T * scale).astype(jnp.bfloat16).reshape(BLOCK, SLOTS, DIM)

            n_grads = BLOCK * b + BLOCK - start

            def give(i, _):
                grad_copy(start + (i + head + 2 * role) % n_grads, push)
                return 0

            lax.fori_loop(0, n_grads, give, 0)
            return 0

        lax.fori_loop(role, last + 1, query_block, 0)

    for i in range(1, 4):
        from_tp = (tp + i) % 4
        arrived(rbuf.at[from_tp], r_rsem.at[from_tp])
    dots = rbuf[0, 0:1, :SLOTS] + rbuf[1, 0:1, :SLOTS] + rbuf[2, 0:1, :SLOTS] + rbuf[3, 0:1, :SLOTS]
    rg_out[...] = jnp.where(valid, gate * (1.0 - gate) * dots, 0.0)

    def collect(h, _):
        arrived(lanes(dqa_out, h), dq_rsem.at[h, 0])

        @pl.when(me >= CUT)
        def _():
            arrived(lanes(dqb_out, h), dq_rsem.at[h, 1])

        arrived(lanes(dk_out, h), dkv_rsem.at[h, 0])
        arrived(lanes(dv_out, h), dkv_rsem.at[h, 1])
        return 0

    lax.fori_loop(0, HEADS, collect, 0)

    outgoing(drain)
    for i in range(1, 4):
        router_copy(i).wait_send()

    @pl.when(y != z)
    def _():
        def end_results(kc, _):
            forward_copies(kc, drain)
            exchange_copy(kc, drain)
            result_copies(kc, drain)
            return 0

        def end_grads(i, _):
            grad_copy(i, drain)
            return 0

        lax.fori_loop(0, n_chunks, end_results, 0)
        lax.fori_loop(first_query, SHARDS // 2, end_grads, 0)


def finish_kernel(dqa, dqb, dk, dv, router, dq_out, dk_out, dv_out, rg_out, buf, in_sems, out_sems):
    me = lax.axis_index("seq")
    parts = [pltpu.make_async_copy(ref, buf.at[i], in_sems.at[i]) for i, ref in enumerate((dk, dv, dqa, dqb))]
    results = [
        pltpu.make_async_copy(buf.at[i], ref, out_sems.at[i]) for i, ref in enumerate((dk_out, dv_out, dq_out))
    ]
    for i in range(3):
        parts[i].start()

    @pl.when(me >= CUT)
    def _():
        parts[3].start()

    rg_out[...] = router[...]
    for i in range(2):
        parts[i].wait()
        results[i].start()
    parts[2].wait()

    @pl.when(me >= CUT)
    def _():
        parts[3].wait()
        buf[2] = (buf[2].astype(jnp.float32) + buf[3].astype(jnp.float32)).astype(jnp.bfloat16)

    results[2].start()
    for result in results:
        result.wait()


def body(q, k, v, o, g, norm, logit, positions):
    low, wide = jnp.bfloat16, jnp.float32
    whole = pl.BlockSpec(memory_space=pltpu.VMEM)
    far = pl.BlockSpec(memory_space=pl.ANY)
    dma = pltpu.SemaphoreType.DMA
    tile = (SLOTS, DIM)
    half = REST // 2
    out = jax.ShapeDtypeStruct((SLOTS, HEADS * DIM), low)
    row = jax.ShapeDtypeStruct((1, SLOTS), wide)
    dqa, dqb, dk, dv, router = pl.pallas_call(
        kernel,
        out_shape=(out, out, out, out, row),
        in_specs=[far, far, far, whole, whole, whole, whole, whole],
        out_specs=(far, far, far, far, whole),
        scratch_shapes=[
            pltpu.VMEM((HEADS,) + tile, low),
            pltpu.VMEM((8 * HEADS + 8, 256), wide),
            pltpu.VMEM((4, 8, 256), wide),
            pltpu.VMEM((REST,) + tile, low),
            pltpu.VMEM((REST,) + tile, low),
            pltpu.VMEM((16,) + tile, low),
            pltpu.VMEM((16,) + tile, low),
            pltpu.VMEM((16, 8, 256), wide),
            pltpu.VMEM((half, 2 * SLOTS, DIM), wide),
            pltpu.VMEM((half, 2 * SLOTS, DIM), wide),
            pltpu.VMEM((half, 2 * SLOTS, DIM), wide),
            pltpu.VMEM((DIM, BLOCK * SLOTS), wide),
            pltpu.VMEM((half, 2) + tile, low),
            pltpu.VMEM((half, 2) + tile, low),
            pltpu.VMEM((half, 2) + tile, low),
            pltpu.VMEM((16,) + tile, low),
            dma((HEADS, 2)),
            dma((HEADS, 2, 3)),
            dma((REST, 2)),
            dma((16, 3)),
            dma((half, 2)),
            dma((half,)),
            dma((half,)),
            dma((half, 2)),
            dma((16,)),
            dma((HEADS, 2)),
            dma((HEADS, 2)),
            dma((4,)),
            dma((4,)),
        ],
        compiler_params=pltpu.CompilerParams(
            collective_id=0, has_side_effects=True, vmem_limit_bytes=56 * 2**20
        ),
        cost_estimate=pl.CostEstimate(flops=9_000_000_000, bytes_accessed=4_000_000, transcendentals=6_000_000),
    )(q, k, v, o, g, norm.T, logit.reshape(1, SLOTS), positions.reshape(-1, DIM))
    dq, dk, dv, router = pl.pallas_call(
        finish_kernel,
        out_shape=(out, out, out, row),
        in_specs=[far, far, far, far, whole],
        out_specs=(far, far, far, whole),
        scratch_shapes=[
            pltpu.VMEM((4, SLOTS, HEADS * DIM), low),
            dma((4,)),
            dma((3,)),
        ],
        compiler_params=pltpu.CompilerParams(vmem_limit_bytes=56 * 2**20),
    )(dqa, dqb, dk, dv, router)
    return dq, dk, dv, router.reshape(SLOTS)


def solution(mesh):
    split = P("seq", "tp")
    return jax.shard_map(
        body,
        mesh=mesh,
        in_specs=(split, split, split, split, split, split, P("seq"), P()),
        out_specs=(split, split, split, P("seq")),
        check_vma=False,
    )
```

```python
import math

import jax
import jax.numpy as jnp
from jax import lax
from jax.experimental import pallas as pl
from jax.experimental.pallas import tpu as pltpu
from jax.sharding import PartitionSpec as P

MESH = pl.DeviceIdType.MESH
LOG2E = math.log2(math.e)
SLOTS = 192
HEADS = 6
DIM = 128
SHARDS = 32
CUT = 12
REST = SHARDS - CUT
BLOCK = 4
FAR = 1e30
NEVER = 1e9


def column(row):
    top = jnp.broadcast_to(row[:, :128], (128, 128)).T
    rest = jnp.concatenate([row[:, 128:], row[:, 128:]], axis=1)
    low = jnp.broadcast_to(rest, (128, 128)).T
    return jnp.concatenate([top, low[:64]], axis=0)


def kernel(
    q_ref, k_hbm, v_hbm, o_ref, g_ref, ln_ref, logit_ref, pos_ref,
    dqa_out, dqb_out, dk_out, dv_out, rg_out,
    dout, stat, rbuf, kbuf, vbuf, qbuf, sbuf, rowid, dkacc, dvacc, dqacc,
    xsend, xrecv, dkvsend, dqsend,
    kv_ssem, q_ssem, kv_rsem, q_rsem, fwd_ssem, x_ssem, x_rsem, dkv_ssem, dq_ssem, dkv_rsem, dq_rsem, r_ssem, r_rsem,
):
    me = lax.axis_index("seq")
    tp = lax.axis_index("tp")
    z, y, c = me // 8, (me // 2) % 4, me % 2
    sibling = me + 1 - 2 * c

    barrier = pltpu.get_barrier_semaphore()

    def greet(i, _):
        pl.semaphore_signal(barrier, inc=1, device_id=((me + i) % SHARDS, tp), device_id_type=MESH)
        return 0

    lax.fori_loop(1, SHARDS, greet, 0)
    for i in range(1, 4):
        pl.semaphore_signal(barrier, inc=1, device_id=(me, (tp + i) % 4), device_id_type=MESH)

    logit = logit_ref[...]
    gate = 1.0 / (1.0 + jnp.exp(-logit))
    at = (me * 3) // 2
    top, low = pos_ref[pl.ds(at, 1), :], pos_ref[pl.ds(at + 1, 1), :]
    even = jnp.concatenate([top, low[:, :64]], axis=1)
    odd = jnp.concatenate([top[:, 64:], low], axis=1)
    valid = jnp.where(c == 0, even, odd) >= 0
    gate_col = column(gate)
    lane = lax.broadcasted_iota(jnp.int32, (SLOTS, DIM), 1)
    table = jnp.zeros((SLOTS, DIM), jnp.float32)
    total = jnp.zeros((SLOTS, 1), jnp.float32)
    for h in range(HEADS):
        grad = g_ref[:, h * DIM : (h + 1) * DIM].astype(jnp.float32)
        wide = o_ref[:, h * DIM : (h + 1) * DIM].astype(jnp.float32)
        low = (gate_col * grad).astype(jnp.bfloat16)
        dout[h, 0] = q_ref[:, h * DIM : (h + 1) * DIM]
        dout[h, 1] = low
        delta = jnp.sum(low.astype(jnp.float32) * wide, axis=1, keepdims=True)
        total += jnp.sum(grad * wide, axis=1, keepdims=True)
        table = jnp.where(lane == 8 * h + 1, delta, table)
    table = jnp.where(lane == 8 * HEADS, total, table)
    flat = jnp.concatenate([table, jnp.zeros((64, DIM), jnp.float32)], axis=0).T
    stat[...] = flat[: 8 * HEADS + 8]
    for h in range(HEADS):
        norm = jnp.where(valid, ln_ref[h : h + 1, :] * LOG2E, FAR)
        stat[8 * h : 8 * h + 1, :SLOTS] = norm
    rbuf[tp] = stat[pl.ds(8 * HEADS, 8), :]

    place = z * 3 + (y - z + 3) % 4
    role = place // HEADS
    head = place % HEADS
    first_key = role * CUT
    n_chunks = jnp.where(role == 0, CUT // 2, REST // 2)

    def chunks_at(b):
        return jnp.where(role == 0, jnp.minimum(4 * b + 4, CUT // 2), jnp.maximum(4 * b - 2, 0))

    @pl.when(y != z)
    def _():
        def make_ids(i, _):
            for j in range(3):
                at = (first_key * 3) // 2 + 3 * i + j
                row = lax.broadcasted_iota(jnp.int32, (1, DIM), 1) + at * DIM
                row = jnp.where(pos_ref[pl.ds(at, 1), :] >= 0, row.astype(jnp.float32), NEVER)
                rowid[i, DIM * j : DIM * (j + 1), :] = jnp.broadcast_to(row, (DIM, DIM)).T
            dkacc[i] = jnp.zeros((2 * SLOTS, DIM), jnp.float32)
            dvacc[i] = jnp.zeros((2 * SLOTS, DIM), jnp.float32)
            return 0

        lax.fori_loop(0, n_chunks, make_ids, 0)

        @pl.when(role == 1)
        def _():
            for i in (CUT // 2 - 2, CUT // 2 - 1):
                qbuf[i] = jnp.zeros((2, SLOTS, DIM), jnp.bfloat16)
                sbuf[i] = jnp.zeros((8, 256), jnp.float32)

    pl.semaphore_wait(barrier, SHARDS - 1 + 3)

    def remote(src, dst, ssem, rsem, to):
        return pltpu.make_async_remote_copy(
            src_ref=src, dst_ref=dst, send_sem=ssem, recv_sem=rsem,
            device_id=(to, tp), device_id_type=MESH,
        )

    def push(src, dst, ssem, rsem, to):
        @pl.when(to == me)
        def _():
            pltpu.make_async_copy(src, dst, rsem).start()

        @pl.when(to != me)
        def _():
            remote(src, dst, ssem, rsem, to).start()

    def drain(src, dst, ssem, rsem, to):
        @pl.when(to != me)
        def _():
            remote(src, dst, ssem, rsem, to).wait_send()

    def arrived(dst, rsem):
        remote(dst, dst, dq_ssem.at[0], rsem, (me + 1) % SHARDS).wait_recv()

    def chip_of(role, h):
        a = role * HEADS + h
        cz = a // 3
        return cz * 8 + ((cz + 1 + a % 3) % 4) * 2

    key_role = (me >= CUT).astype(jnp.int32)
    key_slot = me - CUT * key_role
    query_slot = me // 2

    def lanes(ref, h):
        return ref.at[:, pl.ds(pl.multiple_of(h * DIM, DIM), DIM)]

    def key_copies(h, act):
        to = chip_of(key_role, h) + c
        act(lanes(k_hbm, h), kbuf.at[key_slot], kv_ssem.at[h, 0], kv_rsem.at[key_slot, 0], to)
        act(lanes(v_hbm, h), vbuf.at[key_slot], kv_ssem.at[h, 1], kv_rsem.at[key_slot, 1], to)

    def query_copies(h, role, act):
        to = chip_of(role, h) + c
        act(dout.at[h], qbuf.at[query_slot], q_ssem.at[h, role, 1], q_rsem.at[query_slot, 1], to)
        act(
            stat.at[pl.ds(pl.multiple_of(h * 8, 8), 8), :], sbuf.at[query_slot],
            q_ssem.at[h, role, 2], q_rsem.at[query_slot, 2], to,
        )

    def outgoing(act):
        chip = me // 2

        def keys(i, _):
            key_copies((chip + i) % HEADS, act)
            return 0

        def queries(i, _):
            target = ((chip * 3) // 4 + i) % (2 * HEADS)

            @pl.when((target < HEADS) | (me >= CUT))
            def _():
                query_copies(target % HEADS, target // HEADS, act)

            return 0

        lax.fori_loop(0, HEADS, keys, 0)
        lax.fori_loop(0, 2 * HEADS, queries, 0)

    outgoing(push)

    def router_copy(i):
        return pltpu.make_async_remote_copy(
            src_ref=stat.at[pl.ds(8 * HEADS, 8), :], dst_ref=rbuf.at[tp],
            send_sem=r_ssem.at[i], recv_sem=r_rsem.at[tp],
            device_id=(me, (tp + i) % 4), device_id_type=MESH,
        )

    for i in range(1, 4):
        router_copy(i).start()

    def forward_copies(kc, act):
        slot = 2 * kc + c
        act(kbuf.at[slot], kbuf.at[slot], fwd_ssem.at[kc, 0], kv_rsem.at[slot, 0], sibling)
        act(vbuf.at[slot], vbuf.at[slot], fwd_ssem.at[kc, 1], kv_rsem.at[slot, 1], sibling)

    def exchange_copy(kc, act):
        act(xsend.at[kc], xrecv.at[kc], x_ssem.at[kc], x_rsem.at[kc], sibling)

    def result_copies(kc, act):
        owner = first_key + 2 * kc + c
        act(dkvsend.at[kc, 0], lanes(dk_out, head), dkv_ssem.at[kc, 0], dkv_rsem.at[head, 0], owner)
        act(dkvsend.at[kc, 1], lanes(dv_out, head), dkv_ssem.at[kc, 1], dkv_rsem.at[head, 1], owner)

    def grad_copy(i, act):
        @pl.when(role == 0)
        def _():
            act(dqsend.at[i], lanes(dqa_out, head), dq_ssem.at[i], dq_rsem.at[head, 0], 2 * i + c)

        @pl.when(role == 1)
        def _():
            act(dqsend.at[i], lanes(dqb_out, head), dq_ssem.at[i], dq_rsem.at[head, 1], 2 * i + c)

    scale = DIM ** -0.5
    last = SHARDS // (2 * BLOCK) - 1
    first_query = role * (CUT // 2)

    @pl.when(y != z)
    def _():
        def own_key(kc, _):
            slot = 2 * kc + c
            arrived(kbuf.at[slot], kv_rsem.at[slot, 0])
            arrived(vbuf.at[slot], kv_rsem.at[slot, 1])
            forward_copies(kc, push)
            return 0

        lax.fori_loop(0, n_chunks, own_key, 0)

        def query_block(b, _):
            def wait_query(i, _):
                arrived(qbuf.at[i], q_rsem.at[i, 1])
                arrived(sbuf.at[i], q_rsem.at[i, 2])
                return 0

            def other_key(kc, _):
                slot = 2 * kc + 1 - c
                arrived(kbuf.at[slot], kv_rsem.at[slot, 0])
                arrived(vbuf.at[slot], kv_rsem.at[slot, 1])
                return 0

            before = jnp.where(b == role, 0, chunks_at(b - 1))
            count = chunks_at(b)
            start = jnp.maximum(BLOCK * b, first_query)
            lax.fori_loop(start, BLOCK * b + BLOCK, wait_query, 0)
            lax.fori_loop(before, count, other_key, 0)

            first = pl.ds(BLOCK * b, BLOCK)
            stats = [sbuf[BLOCK * b + j] for j in range(BLOCK)]
            norm_row = jnp.concatenate([s[0:1, :SLOTS] for s in stats], axis=1)
            delta_row = jnp.concatenate([s[1:2, :SLOTS] for s in stats], axis=1)
            step = lax.broadcasted_iota(jnp.int32, (1, SLOTS), 1)
            col_row = jnp.concatenate(
                [(step + (2 * (BLOCK * b + j) + c) * SLOTS).astype(jnp.float32) for j in range(BLOCK)], axis=1
            )
            dqacc[...] = jnp.zeros_like(dqacc)

            def turn(i):
                return (i + (head * count) // HEADS) % count

            def finish(kc):
                mine = pl.ds(pl.multiple_of(c * SLOTS, SLOTS), SLOTS)
                arrived(xrecv.at[kc], x_rsem.at[kc])
                both = dkacc[kc, mine, :] * scale + xrecv[kc, 0].astype(jnp.float32)
                dkvsend[kc, 0] = both.astype(jnp.bfloat16)
                both = dvacc[kc, mine, :] + xrecv[kc, 1].astype(jnp.float32)
                dkvsend[kc, 1] = both.astype(jnp.bfloat16)
                result_copies(kc, push)

            def chunk(i, _):
                kc = turn(i)
                two = pl.ds(2 * kc, 2)
                query = qbuf[first, 0].reshape(BLOCK * SLOTS, DIM)
                grad = qbuf[first, 1].reshape(BLOCK * SLOTS, DIM)
                key = kbuf[two].reshape(2 * SLOTS, DIM)
                value = vbuf[two].reshape(2 * SLOTS, DIM)
                ids = rowid[kc]
                nt = (((1,), (1,)), ((), ()))
                tn = (((0,), (0,)), ((), ()))
                score = lax.dot_general(key, query, nt, preferred_element_type=jnp.float32)
                score = score * (scale * LOG2E) - norm_row
                ids = jnp.concatenate([ids] * (BLOCK * SLOTS // DIM), axis=1)
                prob = jnp.exp2(jnp.where(ids <= col_row, score, -FAR))
                dprob = lax.dot_general(value, grad, nt, preferred_element_type=jnp.float32)
                dscore = (prob * (dprob - delta_row)).astype(jnp.bfloat16)
                prob_low = prob.astype(jnp.bfloat16)
                dvacc[kc] += jnp.dot(prob_low, grad, preferred_element_type=jnp.float32)
                dkacc[kc] += jnp.dot(dscore, query, preferred_element_type=jnp.float32)
                dqacc[...] += lax.dot_general(key, dscore, tn, preferred_element_type=jnp.float32)

                @pl.when(b == last)
                def _():
                    theirs = pl.ds(pl.multiple_of((1 - c) * SLOTS, SLOTS), SLOTS)
                    xsend[kc, 0] = (dkacc[kc, theirs, :] * scale).astype(jnp.bfloat16)
                    xsend[kc, 1] = dvacc[kc, theirs, :].astype(jnp.bfloat16)
                    exchange_copy(kc, push)

                    @pl.when(i > 0)
                    def _():
                        finish(turn(i - 1))

                return 0

            lax.fori_loop(0, count, chunk, 0)

            @pl.when(b == last)
            def _():
                finish(turn(count - 1))

            dqsend[first] = (dqacc[...].T * scale).astype(jnp.bfloat16).reshape(BLOCK, SLOTS, DIM)

            n_grads = BLOCK * b + BLOCK - start

            def give(i, _):
                grad_copy(start + (i + head + 2 * role) % n_grads, push)
                return 0

            lax.fori_loop(0, n_grads, give, 0)
            return 0

        lax.fori_loop(role, last + 1, query_block, 0)

    for i in range(1, 4):
        from_tp = (tp + i) % 4
        arrived(rbuf.at[from_tp], r_rsem.at[from_tp])
    dots = rbuf[0, 0:1, :SLOTS] + rbuf[1, 0:1, :SLOTS] + rbuf[2, 0:1, :SLOTS] + rbuf[3, 0:1, :SLOTS]
    rg_out[...] = jnp.where(valid, gate * (1.0 - gate) * dots, 0.0)

    def collect(h, _):
        arrived(lanes(dqa_out, h), dq_rsem.at[h, 0])

        @pl.when(me >= CUT)
        def _():
            arrived(lanes(dqb_out, h), dq_rsem.at[h, 1])

        arrived(lanes(dk_out, h), dkv_rsem.at[h, 0])
        arrived(lanes(dv_out, h), dkv_rsem.at[h, 1])
        return 0

    lax.fori_loop(0, HEADS, collect, 0)

    outgoing(drain)
    for i in range(1, 4):
        router_copy(i).wait_send()

    @pl.when(y != z)
    def _():
        def end_results(kc, _):
            forward_copies(kc, drain)
            exchange_copy(kc, drain)
            result_copies(kc, drain)
            return 0

        def end_grads(i, _):
            grad_copy(i, drain)
            return 0

        lax.fori_loop(0, n_chunks, end_results, 0)
        lax.fori_loop(first_query, SHARDS // 2, end_grads, 0)


def finish_kernel(dqa, dqb, dk, dv, router, dq_out, dk_out, dv_out, rg_out, buf, in_sems, out_sems):
    me = lax.axis_index("seq")
    parts = [pltpu.make_async_copy(ref, buf.at[i], in_sems.at[i]) for i, ref in enumerate((dk, dv, dqa, dqb))]
    results = [
        pltpu.make_async_copy(buf.at[i], ref, out_sems.at[i]) for i, ref in enumerate((dk_out, dv_out, dq_out))
    ]
    for i in range(3):
        parts[i].start()

    @pl.when(me >= CUT)
    def _():
        parts[3].start()

    rg_out[...] = router[...]
    for i in range(2):
        parts[i].wait()
        results[i].start()
    parts[2].wait()

    @pl.when(me >= CUT)
    def _():
        parts[3].wait()
        buf[2] = (buf[2].astype(jnp.float32) + buf[3].astype(jnp.float32)).astype(jnp.bfloat16)

    results[2].start()
    for result in results:
        result.wait()


def body(q, k, v, o, g, norm, logit, positions):
    low, wide = jnp.bfloat16, jnp.float32
    whole = pl.BlockSpec(memory_space=pltpu.VMEM)
    far = pl.BlockSpec(memory_space=pl.ANY)
    dma = pltpu.SemaphoreType.DMA
    tile = (SLOTS, DIM)
    half = REST // 2
    out = jax.ShapeDtypeStruct((SLOTS, HEADS * DIM), low)
    row = jax.ShapeDtypeStruct((1, SLOTS), wide)
    dqa, dqb, dk, dv, router = pl.pallas_call(
        kernel,
        out_shape=(out, out, out, out, row),
        in_specs=[whole, far, far, whole, whole, whole, whole, whole],
        out_specs=(far, far, far, far, whole),
        scratch_shapes=[
            pltpu.VMEM((HEADS, 2) + tile, low),
            pltpu.VMEM((8 * HEADS + 8, 256), wide),
            pltpu.VMEM((4, 8, 256), wide),
            pltpu.VMEM((REST,) + tile, low),
            pltpu.VMEM((REST,) + tile, low),
            pltpu.VMEM((16, 2) + tile, low),
            pltpu.VMEM((16, 8, 256), wide),
            pltpu.VMEM((half, 2 * SLOTS, DIM), wide),
            pltpu.VMEM((half, 2 * SLOTS, DIM), wide),
            pltpu.VMEM((half, 2 * SLOTS, DIM), wide),
            pltpu.VMEM((DIM, BLOCK * SLOTS), wide),
            pltpu.VMEM((half, 2) + tile, low),
            pltpu.VMEM((half, 2) + tile, low),
            pltpu.VMEM((half, 2) + tile, low),
            pltpu.VMEM((16,) + tile, low),
            dma((HEADS, 2)),
            dma((HEADS, 2, 3)),
            dma((REST, 2)),
            dma((16, 3)),
            dma((half, 2)),
            dma((half,)),
            dma((half,)),
            dma((half, 2)),
            dma((16,)),
            dma((HEADS, 2)),
            dma((HEADS, 2)),
            dma((4,)),
            dma((4,)),
        ],
        compiler_params=pltpu.CompilerParams(
            collective_id=0, has_side_effects=True, vmem_limit_bytes=56 * 2**20
        ),
        cost_estimate=pl.CostEstimate(flops=9_000_000_000, bytes_accessed=4_000_000, transcendentals=6_000_000),
    )(q, k, v, o, g, norm.T, logit.reshape(1, SLOTS), positions.reshape(-1, DIM))
    dq, dk, dv, router = pl.pallas_call(
        finish_kernel,
        out_shape=(out, out, out, row),
        in_specs=[far, far, far, far, whole],
        out_specs=(far, far, far, whole),
        scratch_shapes=[
            pltpu.VMEM((4, SLOTS, HEADS * DIM), low),
            dma((4,)),
            dma((3,)),
        ],
        compiler_params=pltpu.CompilerParams(vmem_limit_bytes=56 * 2**20),
    )(dqa, dqb, dk, dv, router)
    return dq, dk, dv, router.reshape(SLOTS)


def solution(mesh):
    split = P("seq", "tp")
    return jax.shard_map(
        body,
        mesh=mesh,
        in_specs=(split, split, split, split, split, split, P("seq"), P()),
        out_specs=(split, split, split, P("seq")),
        check_vma=False,
    )
```
